32 devices in a mesh: parts: 2 (over x), tp: 16 (over z, y, core).
Axes of the slice: x: 2, y: 2, z: 4, core: 2. Of those that a mesh axis runs over, the one named last changes fastest.
Arguments:
- queries: bfloat16 [64, 16384], P(('parts', 'tp')), parts along dimension 0, may hold values from -40 to 40
- new_token_key_value: bfloat16 [64, 2048], P(('parts', 'tp')), parts along dimension 0, may hold values from -6 to 6
- key_value_cache: bfloat16 [2048, 16, 2048], P(('parts', 'tp')), parts along dimension 0, may hold values from -40 to 40
- row_page_table: int32 [64, 32], P(('parts', 'tp')), parts along dimension 0, may hold values from 0 to 63, as said below
- lengths: int32 [64], P(('parts', 'tp')), parts along dimension 0, may hold values from 1 to 512, as said below
- output_weight_matrix: bfloat16 [16384, 16384], P('tp'), may hold values from -0.0625 to 0.0625
- row_adapter_index: int32 [64, 1], P('parts'), parts along dimension 0, may hold values from 0 to 15; in each aligned block of 32 rows (0 to 31, 32 to 63, ...) at most 4 rows name the same one
- adapter_storage_index: int32 [32], P('parts'), parts along dimension 0, may hold values from 0 to 15, each once
- adapter_down_factor: bfloat16 [32, 64, 16384], P(('parts', 'tp')), parts along dimension 0, may hold values from -0.046875 to 0.046875
- adapter_up_factor: bfloat16 [32, 64, 16384], P(('parts', 'tp')), parts along dimension 0, may hold values from -0.75 to 0.75
Outputs:
- mixed: bfloat16 [64, 16384], P('parts', 'tp'), parts along dimension 0
The draws below stay inside these ranges and needn't reach their ends.
There are 2 independent parts, one for each index of `parts`. The reference program is written for one: setup_inputs(seed, part) draws one part's arguments, and reference() takes and returns one part's arrays. A program takes and returns all parts, laid end to end along the dimension named above; an argument that names none is the same for every part. Nothing has to cross between parts.
Inputs may be any that keep to these rules, and one draw needn't show every extreme that they name: `row_page_table`: the rows held by one device use distinct pages of that device's pool of 64 pages, and every page of the pool. `lengths`: some row has exactly 512 cached tokens. `row_adapter_index`: at most 4 rows name one adapter, a bound that some block reaches; every adapter is named by some row. A permutation: adapter a's factors stand at index adapter_storage_index[a] of adapter_down_factor and adapter_up_factor.
All inputs are finite; a program needn't handle non-finite values.
Results may differ from the reference program's by a relative error of at most 0.009.
Values may be sent and summed in bfloat16 or wider, within the bound.
A program may use at most 128 MiB of HBM per device.

```python
import math
import jax
import jax.numpy as jnp
import numpy as np
from jax import lax

MODEL_WIDTH = 16384
QUERY_HEADS = 128
KVH = 8
HEAD_SIZE = 128
ADAPTER_RANK = 64
ROWS_DEV = 2
PAGE = 16
MAXP = 32
CAP = 4
ROWS = 32
PAGES_DEV = 64
PAGES = 1024
MAXLEN = 512
ADAPTER_SLOTS = 16
N_TP = 16


def draw_queries(key, part):
    key = jax.random.fold_in(key, 5)
    noise_draw = jax.random.normal(key, (ROWS, QUERY_HEADS * HEAD_SIZE), jnp.float32)
    return jnp.clip(noise_draw, -40.0, 40.0).astype(jnp.bfloat16)


def draw_key_value_cache(key, part):
    key = jax.random.fold_in(key, 6)
    noise_draw = jax.random.normal(key, (PAGES, PAGE, KVH, 2, HEAD_SIZE), jnp.float32)
    noise_draw = noise_draw.reshape(PAGES, PAGE, KVH * 2 * HEAD_SIZE)
    return jnp.clip(noise_draw, -40.0, 40.0).astype(jnp.bfloat16)


def draw_row_page_table(key, part):
    key = jax.random.fold_in(key, 8)
    device_keys = jax.random.split(key, N_TP)
    page_orders = jax.vmap(lambda single: jax.random.permutation(single, PAGES_DEV))(device_keys)
    return page_orders.reshape(ROWS, MAXP).astype(jnp.int32)


def draw_lengths(key, part):
    key = jax.random.fold_in(key, 9)
    key_one, key_two = jax.random.split(key)
    length_draw = jax.random.randint(key_one, (ROWS,), 1, MAXLEN + 1, jnp.int32)
    longest_row = jax.random.randint(key_two, (), 0, ROWS, jnp.int32)
    return length_draw.at[longest_row].set(MAXLEN).astype(jnp.int32)


def strengthened(drawn, stream_key, source, target, parts, factor):
    def block_of(axis_at):
        return (jnp.arange(drawn.shape[axis_at]) // (drawn.shape[axis_at] // parts)).reshape((-1,) + (1,) * (drawn.ndim - 1 - axis_at))

    near = jax.random.permutation(stream_key, parts)[block_of(target)]
    second = (block_of(target) + parts // 2) % parts
    return jnp.where((block_of(source) == near) | (block_of(source) == second), factor * drawn, drawn)


def level_of(key, extent, pieces, smallest, high):
    factor_of, own = 1.0, jax.random.fold_in(key, 6)
    for dim, shards_of in pieces:
        steps = jnp.exp(jax.random.uniform(jax.random.fold_in(own, dim), (shards_of,), jnp.float32, smallest / len(pieces), high / len(pieces)))
        factor_of = factor_of * jnp.repeat(steps, extent[dim] // shards_of).reshape([-1 if axis == dim else 1 for axis in range(len(extent))])
    return factor_of


def routed_block(own_key, own, number, rows, number_of, top, limit, skew):
    ranking = jax.random.permutation(own_key, number_of)
    packed, common = shares(number_of, rows * top, limit, skew, True), shares(number_of, rows * top, limit, skew, False)
    places = jnp.arange(number_of)

    def named(sizes, offset_by):
        used = int((sizes > 0).sum())
        fixed = max(1, used // 4)
        shifted = fixed + (places - fixed + offset_by * (used - fixed)) % max(1, number_of - fixed)
        return jnp.zeros((number_of,), jnp.int32).at[ranking[jnp.where(places < fixed, places, shifted)]].set(jnp.asarray(sizes, jnp.int32))

    sizes = jnp.where(number % 4 == 0, named(packed, number // 4), named(common, number - number // 4 - 1))
    mixed = jax.random.permutation(jax.random.fold_in(own, 3), number_of)
    donor, sink = mixed[0:number_of // 2 * 2:2], mixed[1:number_of // 2 * 2:2]
    room = jnp.minimum(sizes[donor] - 1, limit - sizes[sink]) // 2
    room = jnp.where((donor == ranking[0]) | (sink == ranking[0]) | (sizes[sink] == 0), 0, jnp.maximum(room, 0))
    shifted = jax.random.randint(jax.random.fold_in(own, 4), (number_of // 2,), 0, 1 << 20) % (room + 1)
    sizes = sizes.at[donor].add(-shifted).at[sink].add(shifted)
    labels = jnp.searchsorted(jnp.cumsum(sizes), jnp.arange(rows * top), side="right").astype(jnp.int32)
    listing = labels.reshape(top, rows).T
    listing = listing[jax.random.permutation(jax.random.fold_in(own, 1), rows)]
    offset_by = jax.random.randint(jax.random.fold_in(own, 2), (rows, 1), 0, top)
    return jnp.take_along_axis(listing, (jnp.arange(top)[None, :] + offset_by) % top, axis=1)


def shares(amount, total, bound, skew, full):
    portions = [(1 << 20) // math.isqrt(rank ** skew) + 1 for rank in range(1, amount + 1)]
    largest = bound if full else min(bound, max(-(-total // amount), total * portions[0] // sum(portions)))
    least = 1 if total - largest >= amount - 1 else 0
    given, spare = [largest] + [least] * (amount - 1), total - largest - least * (amount - 1)
    while spare > 0:
        movable = [i for i in range(1, amount) if given[i] < largest] or [i for i in range(1, amount) if given[i] < bound]
        mass, budget = sum([portions[i] for i in movable]), spare
        for i in movable:
            addition = min(bound - given[i], max(1, budget * portions[i] // mass), spare)
            given[i] = given[i] + addition
            spare = spare - addition
    return np.array(given)


def normal_values(stream_key, extent, spread, limit, cuts=(), kind=jnp.bfloat16):
    loudness = level_of(stream_key, extent, cuts, -0.22, 0.18) if cuts else 1.0
    result = jax.random.normal(stream_key, extent, jnp.float32) * spread * loudness
    return jnp.minimum(jnp.maximum(result, -limit), limit).astype(kind)


def heavy_noise(own_key, extent, width, bound, cuts, heavy, held_as=jnp.bfloat16):
    values = width * jax.random.normal(own_key, extent, jnp.float32)
    if cuts:
        values = values * level_of(own_key, extent, cuts, -0.22, 0.18)
    return jnp.clip(strengthened(values, jax.random.fold_in(own_key, 3), *heavy), -bound, bound).astype(held_as)


def setup_inputs(seed: int = 0, part: int = 0) -> dict:
    splits = jax.random.split(jax.random.key(seed), 11)
    own_keys = jax.random.split(jax.random.fold_in(splits[10], part), 11)
    queries = draw_queries(jax.random.fold_in(jax.random.fold_in(splits[10], part), 71), part)
    new_token_key_value = normal_values(own_keys[1], (ROWS, KVH * 2 * HEAD_SIZE), 1.0, 6.0, ((0, 16),))
    key_value_cache = draw_key_value_cache(jax.random.fold_in(jax.random.fold_in(splits[10], part), 71), part)
    row_page_table = draw_row_page_table(jax.random.fold_in(jax.random.fold_in(splits[10], part), 71), part)
    lengths = draw_lengths(jax.random.fold_in(jax.random.fold_in(splits[10], part), 71), part)
    output_weight_matrix = heavy_noise(splits[5], (QUERY_HEADS * HEAD_SIZE, MODEL_WIDTH), (QUERY_HEADS * HEAD_SIZE) ** -0.5, 0.0625, ((0, 16),), (0, 1, 16, 2.0))
    row_adapter_index_keys = jax.random.split(jax.random.fold_in(own_keys[6], 1), ROWS // ROWS)
    row_adapter_index_turns = jax.random.permutation(jax.random.fold_in(own_keys[6], 3), ROWS // ROWS)
    row_adapter_index = jax.vmap(lambda own, number: routed_block(jax.random.fold_in(own_keys[6], 2), own, number, ROWS, ADAPTER_SLOTS, 1, CAP, 2))(row_adapter_index_keys, row_adapter_index_turns).reshape((ROWS, 1))
    adapter_storage_index = jax.random.permutation(own_keys[7], ADAPTER_SLOTS).astype(jnp.int32)
    adapter_down_factor = normal_values(own_keys[8], (ADAPTER_SLOTS, ADAPTER_RANK, QUERY_HEADS * HEAD_SIZE), (QUERY_HEADS * HEAD_SIZE) ** -0.5, 0.046875, ((0, 16),))
    adapter_up_factor = normal_values(own_keys[9], (ADAPTER_SLOTS, ADAPTER_RANK, MODEL_WIDTH), ADAPTER_RANK ** -0.5, 0.75, ((0, 16),))
    return dict(queries=queries, new_token_key_value=new_token_key_value, key_value_cache=key_value_cache, row_page_table=row_page_table, lengths=lengths, output_weight_matrix=output_weight_matrix, row_adapter_index=row_adapter_index, adapter_storage_index=adapter_storage_index, adapter_down_factor=adapter_down_factor, adapter_up_factor=adapter_up_factor)


adapter_scale = 2.0


def attend_row(row_query, row_fresh, row_pages, row_length):
    token_count = MAXP * PAGE
    cached = row_pages.reshape(token_count, KVH, 2, HEAD_SIZE)
    joined = jnp.concatenate([cached, row_fresh.reshape(1, KVH, 2, HEAD_SIZE)], axis=0)
    grouped = row_query.reshape(KVH, QUERY_HEADS // KVH, HEAD_SIZE).astype(jnp.float32)
    key_rows = joined[:, :, 0, :].astype(jnp.float32)
    value_rows = joined[:, :, 1, :].astype(jnp.float32)
    scores = jnp.einsum("kgh,lkh->kgl", grouped, key_rows) * (HEAD_SIZE ** -0.5)
    position = jnp.arange(token_count + 1, dtype=jnp.int32)
    visible = (position < row_length) | (position == token_count)
    scores = jnp.where(visible[None, None, :], scores, -1e30)
    row_max = jnp.max(scores, axis=-1, keepdims=True)
    weights = jnp.exp(scores - row_max)
    weights = weights / jnp.sum(weights, axis=-1, keepdims=True)
    weights = lax.optimization_barrier(weights.astype(jnp.bfloat16)).astype(jnp.float32)
    output = jnp.einsum("kgl,lkh->kgh", weights, value_rows)
    return output.reshape(QUERY_HEADS * HEAD_SIZE).astype(jnp.bfloat16)


def reference(queries, new_token_key_value, key_value_cache, row_page_table, lengths, output_weight_matrix, row_adapter_index, adapter_storage_index, adapter_down_factor, adapter_up_factor):
    overall_row_count = queries.shape[0]
    row_device = jnp.arange(overall_row_count, dtype=jnp.int32) // ROWS_DEV
    global_pages = (row_page_table + (row_device * PAGES_DEV)[:, None]).astype(jnp.int32)

    def one_row(position_index):
        return attend_row(queries[position_index], new_token_key_value[position_index], key_value_cache[global_pages[position_index]], lengths[position_index])

    attention_output = lax.map(one_row, jnp.arange(overall_row_count, dtype=jnp.int32))
    base_projection = jnp.dot(attention_output, output_weight_matrix, preferred_element_type=jnp.float32)
    storage_location = adapter_storage_index[row_adapter_index[:, 0]].astype(jnp.int32)

    def adapter_for_row(position_index):
        reduced_output = jnp.dot(adapter_down_factor[storage_location[position_index]], attention_output[position_index], preferred_element_type=jnp.float32)
        reduced_output = reduced_output.astype(jnp.bfloat16)
        adapter_term = jnp.dot(reduced_output, adapter_up_factor[storage_location[position_index]], preferred_element_type=jnp.float32)
        return (adapter_scale * adapter_term).astype(jnp.bfloat16)

    adapter_delta = lax.map(adapter_for_row, jnp.arange(overall_row_count, dtype=jnp.int32))
    return (base_projection + adapter_delta.astype(jnp.float32)).astype(jnp.bfloat16)
```

```python
import functools

import jax
import jax.numpy as jnp
from jax import lax
from jax.experimental import pallas as pl
from jax.experimental.pallas import tpu as pltpu
from jax.sharding import PartitionSpec as P

QUERY_HEADS = 128
KVH = 8
HEAD_SIZE = 128
PAGE = 16
MAXP = 32
CAP = 4
MESH = pl.DeviceIdType.MESH


adapter_scale = 2.0


def fused_kernel(
    n,
    q_ref,
    new_ref,
    kv_hbm,
    table_ref,
    len_ref,
    w_hbm,
    adapter_ref,
    storage_ref,
    down_hbm,
    up_hbm,
    out_ref,
    kv,
    w,
    down,
    up,
    bias,
    send1,
    recv1,
    xf,
    xs,
    send2,
    recv2,
    send3,
    recv3,
    psend,
    precv,
    keep,
    isend,
    irecv,
    kv_sem,
    w_sem,
    f_sem,
    ss1,
    rs1,
    ss2,
    rs2,
    ss3,
    rs3,
    pss,
    prs,
    iss,
    irs,
):
    f32, bf16, i32 = jnp.float32, jnp.bfloat16, jnp.int32
    part = lax.axis_index("parts")
    me = lax.axis_index("tp")
    core = lax.rem(me, 2)
    chip = lax.div(me, 2)
    chips = n // 2
    tokens = kv.shape[1]
    rows = xs.shape[0]
    width = xs.shape[1]

    def to_chip(k):
        return lax.rem(chip + k + 1, chips)

    def kv_copy(g):
        return pltpu.make_async_copy(
            kv_hbm.at[:, pl.ds(pl.multiple_of(g * 256, 256), 256)], kv.at[g], kv_sem.at[g]
        )

    def w_copy(i):
        k, own = lax.div(i, 2), lax.rem(i, 2)
        device = to_chip(k) * 2 + jnp.where(own == 1, core, 1 - core)
        start = pl.multiple_of(device * width, width)
        return pltpu.make_async_copy(w_hbm.at[:, pl.ds(start, width)], w.at[i], w_sem.at[i])

    down_copy = pltpu.make_async_copy(down_hbm, down, f_sem.at[0])
    up_copy = pltpu.make_async_copy(up_hbm, up, f_sem.at[1])

    def loop(low, high, body):
        lax.fori_loop(low, high, lambda i, c: (body(i), c)[1], 0)

    def to_peers(body):
        def one(d):
            @pl.when(d != me)
            def _():
                body(d)

        loop(0, n, one)

    loop(0, KVH, lambda g: kv_copy(g).start())
    loop(0, 8, lambda i: w_copy(i).start())
    down_copy.start()
    up_copy.start()
    loop(8, n, lambda i: w_copy(i).start())

    barrier = pltpu.get_barrier_semaphore()
    to_peers(
        lambda d: pl.semaphore_signal(barrier, inc=1, device_id=(part, d), device_id_type=MESH)
    )

    page = lax.broadcasted_iota(i32, (MAXP, tokens), 1) // PAGE
    slot_at = lax.broadcasted_iota(i32, (MAXP, tokens), 0)
    offset = lax.broadcasted_iota(i32, (MAXP, tokens), 1) % PAGE
    position = (slot_at * PAGE + offset).astype(f32)
    eye = lax.broadcasted_iota(i32, (MAXP, MAXP), 0) == lax.broadcasted_iota(i32, (MAXP, MAXP), 1)
    table = table_ref[...].astype(f32)
    seen = []
    for r in range(2):
        pages = jnp.sum(jnp.where(eye, table[r : r + 1, :], 0.0), axis=1, keepdims=True)
        length = len_ref[r].astype(f32)
        hit = jnp.where((page.astype(f32) == pages) & (position < length), 1.0, 0.0)
        seen.append(jnp.sum(hit, axis=0, keepdims=True))
    row_of = (lax.broadcasted_iota(i32, (32, 1), 0) // 8) % 2
    visible = jnp.where(row_of == 0, seen[0], seen[1])
    bias[...] = jnp.where(visible > 0.5, 0.0, -1e30)

    pl.semaphore_wait(barrier, n - 1)

    def send1_copy(d):
        return pltpu.make_async_remote_copy(
            src_ref=send1.at[d],
            dst_ref=recv1.at[me],
            send_sem=ss1.at[d],
            recv_sem=rs1.at[me],
            device_id=(part, d),
            device_id_type=MESH,
        )

    scale = HEAD_SIZE ** (-0.5)

    def attend(g):
        kv_copy(g).wait()
        query = q_ref[pl.ds(pl.multiple_of(g * 32, 32), 32), :]
        keys = kv[g, :, 0:128]
        scores = lax.dot_general(query, keys, (((1,), (1,)), ((), ())), preferred_element_type=f32)
        scores = scores * scale + bias[...]
        fresh = new_ref[:, pl.ds(pl.multiple_of(g * 256, 256), 256)].astype(f32)
        fresh = jnp.where(row_of == 0, fresh[0:1], fresh[1:2])
        fresh_score = jnp.sum(query.astype(f32) * fresh[:, :128], axis=1, keepdims=True) * scale
        top = jnp.maximum(jnp.max(scores, axis=1, keepdims=True), fresh_score)
        grown = jnp.exp(scores - top)
        fresh_grown = jnp.exp(fresh_score - top)
        inverse = 1.0 / (jnp.sum(grown, axis=1, keepdims=True) + fresh_grown)
        weights = (grown * inverse).astype(bf16)
        fresh_weight = (fresh_grown * inverse).astype(bf16).astype(f32)
        attended = jnp.dot(weights, kv[g, :, 128:256], preferred_element_type=f32)
        attended = (attended + fresh_weight * fresh[:, 128:]).astype(bf16)
        for half in range(2):
            d = g * 2 + half
            send1[d] = attended[half * 16 : half * 16 + 16]

            @pl.when(d != me)
            def _():
                send1_copy(d).start()

    loop(0, KVH, attend)

    lane = lax.broadcasted_iota(i32, (rows, 128), 1) % rows
    sub = lax.broadcasted_iota(i32, (rows, 128), 0)
    owner_row = jnp.zeros((rows, 128), i32)
    owner_column = jnp.zeros((rows, 128), i32)
    for r in range(rows):
        owner = storage_ref[adapter_ref[r, 0]]
        owner_row = jnp.where(lane == r, owner, owner_row)
        owner_column = jnp.where(sub == r, owner, owner_column)
    same = owner_row == owner_column
    first = lax.broadcasted_iota(i32, (rows, 128), 1) < rows
    rank_row = jnp.sum(jnp.where(same & (sub < lane), 1.0, 0.0), axis=0, keepdims=True)
    rank_column = jnp.sum(jnp.where(same & (lane < sub) & first, 1.0, 0.0), axis=1, keepdims=True)
    slot_row = owner_row[0:1].astype(f32) * CAP + rank_row
    slot_column = owner_column[:, 0:1].astype(f32) * CAP + rank_column
    at = lax.broadcasted_iota(i32, (n * 16, 128), 0)
    quarter_at = lax.broadcasted_iota(i32, (n * 16, 128), 1) // rows
    wanted = ((at // 16) * CAP + at % CAP).astype(f32)
    place = jnp.where((wanted == slot_row) & ((at // CAP) % 4 == quarter_at), 1.0, 0.0).astype(bf16)

    recv1[me] = send1[me]
    to_peers(lambda d: pltpu.make_async_remote_copy(
        src_ref=send1.at[d],
        dst_ref=recv1.at[d],
        send_sem=ss1.at[d],
        recv_sem=rs1.at[d],
        device_id=(part, d),
        device_id_type=MESH,
    ).wait_recv())
    xf[...] = recv1[...].reshape(n * 16, 128).astype(f32)
    x = jnp.concatenate([xf[pl.ds(h, rows, stride=8), :] for h in range(8)], axis=1).astype(bf16)
    xs[...] = x

    def copy_of(send, recv, ss, rs, d, landing):
        return pltpu.make_async_remote_copy(
            src_ref=send.at[d],
            dst_ref=recv.at[landing],
            send_sem=ss.at[d],
            recv_sem=rs.at[landing],
            device_id=(part, d),
            device_id_type=MESH,
        )

    stacked = jnp.concatenate([x[:, i * 256 : i * 256 + 256] for i in range(4)], axis=0)
    picked = jnp.dot(place, stacked, preferred_element_type=f32).astype(bf16)
    send2[...] = picked.reshape(n, 16, 256)
    to_peers(lambda d: copy_of(send2, recv2, ss2, rs2, d, me).start())
    recv2[me] = send2[me]

    def partner_copy(k):
        return pltpu.make_async_remote_copy(
            src_ref=psend.at[k],
            dst_ref=precv.at[k],
            send_sem=pss.at[k],
            recv_sem=prs.at[k],
            device_id=(part, chip * 2 + 1 - core),
            device_id_type=MESH,
        )

    def chip_copy(k):
        return pltpu.make_async_remote_copy(
            src_ref=isend.at[k],
            dst_ref=irecv.at[k],
            send_sem=iss.at[k],
            recv_sem=irs.at[k],
            device_id=(part, to_chip(k) * 2 + core),
            device_id_type=MESH,
        )

    def multiply(k):
        for own, into in ((0, psend), (1, keep)):
            w_copy(k * 2 + own).wait()
            for c in range(0, width, 512):
                into[k, :, c : c + 512] = jnp.dot(
                    xs[...], w[k * 2 + own, :, c : c + 512], preferred_element_type=f32
                )
            if own == 0:
                partner_copy(k).start()

    def finish(k):
        partner_copy(k).wait_recv()
        isend[k] = (keep[k] + precv[k]).astype(bf16)
        chip_copy(k).start()

    def step(k):
        multiply(k)
        finish(k - 1)

    multiply(0)
    loop(1, 4, step)

    down_copy.wait()
    up_copy.wait()
    to_peers(lambda d: copy_of(send2, recv2, ss2, rs2, d, d).wait_recv())
    quarter = lax.broadcasted_iota(i32, (16, 256), 0) // CAP

    def reduce_one(s, total):
        piece = recv2[s].astype(f32)
        spread = jnp.concatenate(
            [jnp.where(quarter == i, piece, 0.0) for i in range(4)], axis=1
        ).astype(bf16)
        factor = down[:, pl.ds(pl.multiple_of(s * width, width), width)]
        return total + lax.dot_general(
            spread, factor, (((1,), (1,)), ((), ())), preferred_element_type=f32
        )

    total = lax.fori_loop(0, n, reduce_one, jnp.zeros((16, down.shape[0]), f32))
    summed = total[0:4] + total[4:8] + total[8:12] + total[12:16]
    reduced = jnp.concatenate([summed] * 4, axis=0).astype(bf16)

    def raise_one(d):
        factor = up[:, pl.ds(pl.multiple_of(d * width, width), width)]
        term = adapter_scale * jnp.dot(reduced, factor, preferred_element_type=f32)
        piece = jnp.zeros((16, 256), f32)
        for i in range(4):
            piece = jnp.where(quarter == i, term[:, i * 256 : i * 256 + 256], piece)
        send3[d] = piece.astype(bf16)

        @pl.when(d != me)
        def _():
            copy_of(send3, recv3, ss3, rs3, d, me).start()

    loop(0, n, raise_one)
    recv3[me] = send3[me]

    loop(4, chips, step)

    to_peers(lambda d: copy_of(send3, recv3, ss3, rs3, d, d).wait_recv())
    back = lax.broadcasted_iota(i32, (rows, n * 16), 1)
    named = ((back // 16) * CAP + back % CAP).astype(f32) == slot_column
    deltas = recv3[...].reshape(n * 16, 256)
    last = chips - 1
    partner_copy(last).wait_recv()
    result = keep[last] + precv[last]
    result = result + jnp.concatenate(
        [
            jnp.dot(
                jnp.where(named & ((back // CAP) % 4 == i), 1.0, 0.0).astype(bf16),
                deltas,
                preferred_element_type=f32,
            )
            for i in range(4)
        ],
        axis=1,
    )
    for k in range(chips - 1):
        chip_copy(k).wait_recv()
        result = result + irecv[k].astype(f32)
    out_ref[...] = result.astype(bf16)

    def sent(d):
        copy_of(send1, recv1, ss1, rs1, d, me).wait_send()
        copy_of(send2, recv2, ss2, rs2, d, me).wait_send()
        copy_of(send3, recv3, ss3, rs3, d, me).wait_send()

    to_peers(sent)
    loop(0, chips, lambda k: partner_copy(k).wait_send())
    loop(0, chips - 1, lambda k: chip_copy(k).wait_send())


def fused_body(
    n,
    queries,
    new_token_key_value,
    key_value_cache,
    row_page_table,
    lengths,
    output_weight_matrix,
    row_adapter_index,
    adapter_storage_index,
    adapter_down_factor,
    adapter_up_factor,
):
    rows = row_adapter_index.shape[0]
    width = output_weight_matrix.shape[0]
    tokens = key_value_cache.shape[0] * PAGE
    rank = adapter_down_factor.shape[1]
    features = queries.shape[1]
    chips = n // 2
    heads = queries.reshape(2, n, 8, HEAD_SIZE).transpose(1, 0, 2, 3).reshape(n * 16, HEAD_SIZE)
    bf16, f32 = jnp.bfloat16, jnp.float32
    vmem = pl.BlockSpec(memory_space=pltpu.VMEM)
    smem = pl.BlockSpec(memory_space=pltpu.SMEM)
    hbm = pl.BlockSpec(memory_space=pl.ANY)
    dma = pltpu.SemaphoreType.DMA
    return pl.pallas_call(
        functools.partial(fused_kernel, n),
        out_shape=jax.ShapeDtypeStruct((rows, width), bf16),
        in_specs=[vmem, vmem, hbm, vmem, smem, hbm, smem, smem, hbm, hbm],
        out_specs=vmem,
        scratch_shapes=[
            pltpu.VMEM((KVH, tokens, 256), bf16),
            pltpu.VMEM((n, width, width), bf16),
            pltpu.VMEM((rank, features), bf16),
            pltpu.VMEM((rank, features), bf16),
            pltpu.VMEM((32, tokens), f32),
            pltpu.VMEM((n, 16, 128), bf16),
            pltpu.VMEM((n, 16, 128), bf16),
            pltpu.VMEM((n * 16, 128), f32),
            pltpu.VMEM((rows, width), bf16),
            pltpu.VMEM((n, 16, 256), bf16),
            pltpu.VMEM((n, 16, 256), bf16),
            pltpu.VMEM((n, 16, 256), bf16),
            pltpu.VMEM((n, 16, 256), bf16),
            pltpu.VMEM((chips, rows, width), f32),
            pltpu.VMEM((chips, rows, width), f32),
            pltpu.VMEM((chips, rows, width), f32),
            pltpu.VMEM((chips, rows, width), bf16),
            pltpu.VMEM((chips, rows, width), bf16),
            dma((KVH,)),
            dma((n,)),
            dma((2,)),
            dma((n,)),
            dma((n,)),
            dma((n,)),
            dma((n,)),
            dma((n,)),
            dma((n,)),
            dma((chips,)),
            dma((chips,)),
            dma((chips,)),
            dma((chips,)),
        ],
        compiler_params=pltpu.CompilerParams(
            collective_id=0, has_side_effects=True, vmem_limit_bytes=56 * 1024 * 1024
        ),
    )(
        heads,
        new_token_key_value,
        key_value_cache.reshape(tokens, key_value_cache.shape[2]),
        row_page_table,
        lengths,
        output_weight_matrix,
        row_adapter_index,
        adapter_storage_index,
        adapter_down_factor.reshape(rank, features),
        adapter_up_factor.reshape(rank, features),
    )


def attend_rows(queries, new_token_key_value, gathered_pages, lengths):
    local_rows = queries.shape[0]
    token_count = MAXP * PAGE
    group_size = QUERY_HEADS // KVH
    grouped = queries.reshape(local_rows, KVH, group_size, HEAD_SIZE)
    cached = gathered_pages.reshape(local_rows, token_count, KVH, 2, HEAD_SIZE)
    fresh = new_token_key_value.reshape(local_rows, KVH, 2, HEAD_SIZE)
    scale_factor = HEAD_SIZE ** (-0.5)
    scores = (
        jnp.einsum(
            "rkgh,rlkh->rkgl", grouped, cached[:, :, :, 0, :], preferred_element_type=jnp.float32
        )
        * scale_factor
    )
    fresh_score = (
        jnp.einsum("rkgh,rkh->rkg", grouped, fresh[:, :, 0, :], preferred_element_type=jnp.float32)
        * scale_factor
    )
    position = jnp.arange(token_count, dtype=jnp.int32)
    visible = position[None, :] < lengths[:, None]
    scores = jnp.where(visible[:, None, None, :], scores, -1e30)
    row_max = jnp.maximum(jnp.max(scores, axis=-1), fresh_score)
    cached_exp = jnp.exp(scores - row_max[..., None])
    fresh_exp = jnp.exp(fresh_score - row_max)
    total = jnp.sum(cached_exp, axis=-1) + fresh_exp
    weights = (cached_exp / total[..., None]).astype(jnp.bfloat16)
    fresh_weight = (fresh_exp / total).astype(jnp.bfloat16)
    output = jnp.einsum(
        "rkgl,rlkh->rkgh", weights, cached[:, :, :, 1, :], preferred_element_type=jnp.float32
    )
    output = output + fresh_weight.astype(jnp.float32)[..., None] * fresh[:, :, None, 1, :].astype(
        jnp.float32
    )
    return output.reshape(local_rows, QUERY_HEADS * HEAD_SIZE).astype(jnp.bfloat16)


def body(
    queries,
    new_token_key_value,
    key_value_cache,
    row_page_table,
    lengths,
    output_weight_matrix,
    row_adapter_index,
    adapter_storage_index,
    adapter_down_factor,
    adapter_up_factor,
):
    gathered_pages = key_value_cache[row_page_table]
    attention_output = attend_rows(queries, new_token_key_value, gathered_pages, lengths)
    head_rows = lax.all_to_all(attention_output, "tp", split_axis=1, concat_axis=0, tiled=True)
    partial_value = jnp.dot(head_rows, output_weight_matrix, preferred_element_type=jnp.float32)
    base_projection = lax.psum_scatter(partial_value, "tp", scatter_dimension=1, tiled=True)
    row_adapter = row_adapter_index[:, 0]
    row_owner = adapter_storage_index[row_adapter]
    down_slices, up_slices = (
        lax.all_to_all(adapter_down_factor, "tp", split_axis=2, concat_axis=0, tiled=True),
        lax.all_to_all(adapter_up_factor, "tp", split_axis=2, concat_axis=0, tiled=True),
    )
    picked = down_slices[row_owner]
    partial_low = jnp.einsum("rh,rkh->rk", head_rows, picked, preferred_element_type=jnp.float32)
    reduced_output = lax.psum(partial_low, "tp").astype(jnp.bfloat16)
    adapter_term = jnp.einsum(
        "rk,rkd->rd", reduced_output, up_slices[row_owner], preferred_element_type=jnp.float32
    )
    adapter_delta = (adapter_scale * adapter_term).astype(jnp.bfloat16)
    return (base_projection + adapter_delta.astype(jnp.float32)).astype(jnp.bfloat16)


def solution(mesh):
    in_specs = (
        P(("parts", "tp"), None),
        P(("parts", "tp"), None),
        P(("parts", "tp"), None, None),
        P(("parts", "tp"), None),
        P(("parts", "tp")),
        P("tp", None),
        P("parts", None),
        P("parts"),
        P(("parts", "tp"), None, None),
        P(("parts", "tp"), None, None),
    )
    out_specs = P("parts", "tp")
    n = mesh.shape["tp"]
    run = functools.partial(fused_body, n) if n == 16 else body
    return jax.shard_map(run, mesh=mesh, in_specs=in_specs, out_specs=out_specs, check_vma=False)
```

```python
import functools

import jax
import jax.numpy as jnp
from jax import lax
from jax.experimental import pallas as pl
from jax.experimental.pallas import tpu as pltpu
from jax.sharding import PartitionSpec as P

QUERY_HEADS = 128
KVH = 8
HEAD_SIZE = 128
PAGE = 16
MAXP = 32
CAP = 4
MESH = pl.DeviceIdType.MESH


adapter_scale = 2.0


def fused_kernel(
    n,
    q_ref,
    new_ref,
    kv_hbm,
    table_ref,
    len_ref,
    w_hbm,
    adapter_ref,
    storage_ref,
    down_hbm,
    up_hbm,
    out_ref,
    kv,
    w,
    down,
    up,
    bias,
    qs,
    send1,
    recv1,
    xf,
    xs,
    send2,
    recv2,
    send3,
    recv3,
    psend,
    precv,
    keep,
    ysend,
    yrecv,
    isend,
    irecv,
    kv_sem,
    w_sem,
    f_sem,
    ss1,
    rs1,
    ss2,
    rs2,
    ss3,
    rs3,
    pss,
    prs,
    yss,
    yrs,
    iss,
    irs,
):
    f32, bf16, i32 = jnp.float32, jnp.bfloat16, jnp.int32
    part = lax.axis_index("parts")
    me = lax.axis_index("tp")
    core = lax.rem(me, 2)
    chip = lax.div(me, 2)
    depth, across = lax.div(chip, 2), lax.rem(chip, 2)
    chips = n // 2
    depths = chips // 2
    tokens = kv.shape[1]
    rows = xs.shape[0]
    width = xs.shape[1]

    def to_depth(k):
        return lax.rem(depth + k + 1, depths)

    def to_chip(k):
        near = lax.div(k, depths) == 1
        return to_depth(lax.rem(k, depths)) * 2 + jnp.where(near, across, 1 - across)

    def kv_copy(g):
        return pltpu.make_async_copy(
            kv_hbm.at[:, pl.ds(pl.multiple_of(g * 256, 256), 256)], kv.at[g], kv_sem.at[g]
        )

    def w_copy(i):
        k, own = lax.div(i, 2), lax.rem(i, 2)
        device = to_chip(k) * 2 + jnp.where(own == 1, core, 1 - core)
        start = pl.multiple_of(device * width, width)
        return pltpu.make_async_copy(w_hbm.at[:, pl.ds(start, width)], w.at[i], w_sem.at[i])

    down_copy = pltpu.make_async_copy(down_hbm, down, f_sem.at[0])
    up_copy = pltpu.make_async_copy(up_hbm, up, f_sem.at[1])

    def loop(low, high, body):
        lax.fori_loop(low, high, lambda i, c: (body(i), c)[1], 0)

    def to_peers(body):
        def one(d):
            @pl.when(d != me)
            def _():
                body(d)

        loop(0, n, one)

    loop(0, KVH, lambda g: kv_copy(g).start())
    barrier = pltpu.get_barrier_semaphore()
    to_peers(
        lambda d: pl.semaphore_signal(barrier, inc=1, device_id=(part, d), device_id_type=MESH)
    )

    loop(0, 8, lambda i: w_copy(i).start())
    down_copy.start()
    up_copy.start()
    loop(8, n, lambda i: w_copy(i).start())

    page = lax.broadcasted_iota(i32, (MAXP, tokens), 1) // PAGE
    slot_at = lax.broadcasted_iota(i32, (MAXP, tokens), 0)
    offset = lax.broadcasted_iota(i32, (MAXP, tokens), 1) % PAGE
    position = (slot_at * PAGE + offset).astype(f32)
    eye = lax.broadcasted_iota(i32, (MAXP, MAXP), 0) == lax.broadcasted_iota(i32, (MAXP, MAXP), 1)
    table = table_ref[...].astype(f32)
    seen = []
    for r in range(2):
        pages = jnp.sum(jnp.where(eye, table[r : r + 1, :], 0.0), axis=1, keepdims=True)
        length = len_ref[r].astype(f32)
        hit = jnp.where((page.astype(f32) == pages) & (position < length), 1.0, 0.0)
        seen.append(jnp.sum(hit, axis=0, keepdims=True))
    row_of = (lax.broadcasted_iota(i32, (32, 1), 0) // 8) % 2
    visible = jnp.where(row_of == 0, seen[0], seen[1])
    bias[...] = jnp.where(visible > 0.5, 0.0, -1e30)

    for h in range(n * 8):
        at_row = (h // 8) * 16 + h % 8
        qs[pl.ds(at_row, 2, stride=8), :] = q_ref[:, h * 128 : h * 128 + 128].astype(f32)

    def send1_copy(d):
        return pltpu.make_async_remote_copy(
            src_ref=send1.at[d],
            dst_ref=recv1.at[me],
            send_sem=ss1.at[d],
            recv_sem=rs1.at[me],
            device_id=(part, d),
            device_id_type=MESH,
        )

    scale = HEAD_SIZE ** (-0.5)

    def attend(g):
        kv_copy(g).wait()
        query = qs[pl.ds(pl.multiple_of(g * 32, 32), 32), :].astype(bf16)
        keys = kv[g, :, 0:128]
        scores = lax.dot_general(query, keys, (((1,), (1,)), ((), ())), preferred_element_type=f32)
        scores = scores * scale + bias[...]
        fresh = new_ref[:, pl.ds(pl.multiple_of(g * 256, 256), 256)].astype(f32)
        fresh = jnp.where(row_of == 0, fresh[0:1], fresh[1:2])
        fresh_score = jnp.sum(query.astype(f32) * fresh[:, :128], axis=1, keepdims=True) * scale
        top = jnp.maximum(jnp.max(scores, axis=1, keepdims=True), fresh_score)
        grown = jnp.exp(scores - top)
        fresh_grown = jnp.exp(fresh_score - top)
        inverse = 1.0 / (jnp.sum(grown, axis=1, keepdims=True) + fresh_grown)
        weights = (grown * inverse).astype(bf16)
        fresh_weight = (fresh_grown * inverse).astype(bf16).astype(f32)
        attended = jnp.dot(weights, kv[g, :, 128:256], preferred_element_type=f32)
        attended = (attended + fresh_weight * fresh[:, 128:]).astype(bf16)
        for half in range(2):
            d = g * 2 + half
            send1[d] = attended[half * 16 : half * 16 + 16]

    loop(0, KVH, attend)
    pl.semaphore_wait(barrier, n - 1)
    to_peers(lambda d: send1_copy(d).start())

    lane = lax.broadcasted_iota(i32, (rows, 128), 1) % rows
    sub = lax.broadcasted_iota(i32, (rows, 128), 0)
    owner_row = jnp.zeros((rows, 128), i32)
    owner_column = jnp.zeros((rows, 128), i32)
    for r in range(rows):
        owner = storage_ref[adapter_ref[r]]
        owner_row = jnp.where(lane == r, owner, owner_row)
        owner_column = jnp.where(sub == r, owner, owner_column)
    same = owner_row == owner_column
    first = lax.broadcasted_iota(i32, (rows, 128), 1) < rows
    rank_row = jnp.sum(jnp.where(same & (sub < lane), 1.0, 0.0), axis=0, keepdims=True)
    rank_column = jnp.sum(jnp.where(same & (lane < sub) & first, 1.0, 0.0), axis=1, keepdims=True)
    slot_row = owner_row[0:1].astype(f32) * CAP + rank_row
    slot_column = owner_column[:, 0:1].astype(f32) * CAP + rank_column
    at = lax.broadcasted_iota(i32, (n * 16, 128), 0)
    quarter_at = lax.broadcasted_iota(i32, (n * 16, 128), 1) // rows
    wanted = ((at // 16) * CAP + at % CAP).astype(f32)
    place = jnp.where((wanted == slot_row) & ((at // CAP) % 4 == quarter_at), 1.0, 0.0).astype(bf16)

    recv1[me] = send1[me]
    to_peers(lambda d: pltpu.make_async_remote_copy(
        src_ref=send1.at[d],
        dst_ref=recv1.at[d],
        send_sem=ss1.at[d],
        recv_sem=rs1.at[d],
        device_id=(part, d),
        device_id_type=MESH,
    ).wait_recv())
    xf[...] = recv1[...].reshape(n * 16, 128).astype(f32)
    x = jnp.concatenate([xf[pl.ds(h, rows, stride=8), :] for h in range(8)], axis=1).astype(bf16)
    xs[...] = x

    def copy_of(send, recv, ss, rs, d, landing):
        return pltpu.make_async_remote_copy(
            src_ref=send.at[d],
            dst_ref=recv.at[landing],
            send_sem=ss.at[d],
            recv_sem=rs.at[landing],
            device_id=(part, d),
            device_id_type=MESH,
        )

    stacked = jnp.concatenate([x[:, i * 256 : i * 256 + 256] for i in range(4)], axis=0)
    picked = jnp.dot(place, stacked, preferred_element_type=f32).astype(bf16)
    send2[...] = picked.reshape(n, 16, 256)
    to_peers(lambda d: copy_of(send2, recv2, ss2, rs2, d, me).start())
    recv2[me] = send2[me]

    def partner_copy(k):
        return pltpu.make_async_remote_copy(
            src_ref=psend.at[k],
            dst_ref=precv.at[k],
            send_sem=pss.at[k],
            recv_sem=prs.at[k],
            device_id=(part, chip * 2 + 1 - core),
            device_id_type=MESH,
        )

    def across_copy(k):
        return pltpu.make_async_remote_copy(
            src_ref=ysend.at[k],
            dst_ref=yrecv.at[k],
            send_sem=yss.at[k],
            recv_sem=yrs.at[k],
            device_id=(part, (depth * 2 + 1 - across) * 2 + core),
            device_id_type=MESH,
        )

    def depth_copy(k):
        return pltpu.make_async_remote_copy(
            src_ref=isend.at[k],
            dst_ref=irecv.at[k],
            send_sem=iss.at[k],
            recv_sem=irs.at[k],
            device_id=(part, (to_depth(k) * 2 + across) * 2 + core),
            device_id_type=MESH,
        )

    def multiply(k):
        for own, into in ((0, psend), (1, keep)):
            w_copy(k * 2 + own).wait()
            for c in range(0, width, 512):
                into[k, :, c : c + 512] = jnp.dot(
                    xs[...], w[k * 2 + own, :, c : c + 512], preferred_element_type=f32
                )
            if own == 0:
                partner_copy(k).start()

    def sum_far(k):
        partner_copy(k).wait_recv()
        ysend[k] = (keep[k] + precv[k]).astype(bf16)
        across_copy(k).start()

    def sum_near(k):
        partner_copy(depths + k).wait_recv()
        across_copy(k).wait_recv()
        return keep[depths + k] + precv[depths + k] + yrecv[k].astype(f32)

    def send_depth(k):
        isend[k] = sum_near(k).astype(bf16)
        depth_copy(k).start()

    def far_step(k):
        multiply(k)
        sum_far(k - 1)

    def near_step(k):
        multiply(depths + k)
        send_depth(k - 1)

    multiply(0)
    loop(1, depths + 1, far_step)
    loop(1, depths - 1, near_step)

    down_copy.wait()
    up_copy.wait()
    to_peers(lambda d: copy_of(send2, recv2, ss2, rs2, d, d).wait_recv())
    quarter = lax.broadcasted_iota(i32, (16, 256), 0) // CAP

    def reduce_one(s, total):
        piece = recv2[s].astype(f32)
        spread = jnp.concatenate(
            [jnp.where(quarter == i, piece, 0.0) for i in range(4)], axis=1
        ).astype(bf16)
        factor = down[:, pl.ds(pl.multiple_of(s * width, width), width)]
        return total + lax.dot_general(
            spread, factor, (((1,), (1,)), ((), ())), preferred_element_type=f32
        )

    total = lax.fori_loop(0, n, reduce_one, jnp.zeros((16, down.shape[0]), f32), unroll=4)
    summed = total[0:4] + total[4:8] + total[8:12] + total[12:16]
    reduced = jnp.concatenate([summed] * 4, axis=0).astype(bf16)

    send_depth(depths - 2)

    def raise_four(start):
        for d in [start * 4 + i for i in range(4)]:
            factor = up[:, pl.ds(pl.multiple_of(d * width, width), width)]
            term = adapter_scale * jnp.dot(reduced, factor, preferred_element_type=f32)
            piece = jnp.zeros((16, 256), f32)
            for i in range(4):
                piece = jnp.where(quarter == i, term[:, i * 256 : i * 256 + 256], piece)
            send3[d] = piece.astype(bf16)
        for d in [start * 4 + i for i in range(4)]:

            @pl.when(d != me)
            def _():
                copy_of(send3, recv3, ss3, rs3, d, me).start()

    loop(0, n // 4, raise_four)
    recv3[me] = send3[me]
    multiply(chips - 1)
    result = sum_near(depths - 1)
    for k in range(depths - 1):
        depth_copy(k).wait_recv()
        result = result + irecv[k].astype(f32)

    to_peers(lambda d: copy_of(send3, recv3, ss3, rs3, d, d).wait_recv())
    back = lax.broadcasted_iota(i32, (rows, n * 16), 1)
    named = ((back // 16) * CAP + back % CAP).astype(f32) == slot_column
    deltas = recv3[...].reshape(n * 16, 256)
    result = result + jnp.concatenate(
        [
            jnp.dot(
                jnp.where(named & ((back // CAP) % 4 == i), 1.0, 0.0).astype(bf16),
                deltas,
                preferred_element_type=f32,
            )
            for i in range(4)
        ],
        axis=1,
    )
    out_ref[...] = result.astype(bf16)

    def sent(d):
        copy_of(send1, recv1, ss1, rs1, d, me).wait_send()
        copy_of(send2, recv2, ss2, rs2, d, me).wait_send()
        copy_of(send3, recv3, ss3, rs3, d, me).wait_send()

    to_peers(sent)
    loop(0, chips, lambda k: partner_copy(k).wait_send())
    loop(0, depths, lambda k: across_copy(k).wait_send())
    loop(0, depths - 1, lambda k: depth_copy(k).wait_send())


def fused_body(
    n,
    queries,
    new_token_key_value,
    key_value_cache,
    row_page_table,
    lengths,
    output_weight_matrix,
    row_adapter_index,
    adapter_storage_index,
    adapter_down_factor,
    adapter_up_factor,
):
    rows = row_adapter_index.shape[0]
    width = output_weight_matrix.shape[0]
    tokens = key_value_cache.shape[0] * PAGE
    rank = adapter_down_factor.shape[1]
    features = queries.shape[1]
    chips = n // 2
    bf16, f32 = jnp.bfloat16, jnp.float32
    vmem = pl.BlockSpec(memory_space=pltpu.VMEM)
    smem = pl.BlockSpec(memory_space=pltpu.SMEM)
    hbm = pl.BlockSpec(memory_space=pl.ANY)
    dma = pltpu.SemaphoreType.DMA
    return pl.pallas_call(
        functools.partial(fused_kernel, n),
        out_shape=jax.ShapeDtypeStruct((rows, width), bf16),
        in_specs=[vmem, vmem, hbm, vmem, smem, hbm, smem, smem, hbm, hbm],
        out_specs=vmem,
        scratch_shapes=[
            pltpu.VMEM((KVH, tokens, 256), bf16),
            pltpu.VMEM((n, width, width), bf16),
            pltpu.VMEM((rank, features), bf16),
            pltpu.VMEM((rank, features), bf16),
            pltpu.VMEM((32, tokens), f32),
            pltpu.VMEM((n * 16, 128), f32),
            pltpu.VMEM((n, 16, 128), bf16),
            pltpu.VMEM((n, 16, 128), bf16),
            pltpu.VMEM((n * 16, 128), f32),
            pltpu.VMEM((rows, width), bf16),
            pltpu.VMEM((n, 16, 256), bf16),
            pltpu.VMEM((n, 16, 256), bf16),
            pltpu.VMEM((n, 16, 256), bf16),
            pltpu.VMEM((n, 16, 256), bf16),
            pltpu.VMEM((chips, rows, width), f32),
            pltpu.VMEM((chips, rows, width), f32),
            pltpu.VMEM((chips, rows, width), f32),
            pltpu.VMEM((chips // 2, rows, width), bf16),
            pltpu.VMEM((chips // 2, rows, width), bf16),
            pltpu.VMEM((chips // 2, rows, width), bf16),
            pltpu.VMEM((chips // 2, rows, width), bf16),
            dma((KVH,)),
            dma((n,)),
            dma((2,)),
            dma((n,)),
            dma((n,)),
            dma((n,)),
            dma((n,)),
            dma((n,)),
            dma((n,)),
            dma((chips,)),
            dma((chips,)),
            dma((chips // 2,)),
            dma((chips // 2,)),
            dma((chips // 2,)),
            dma((chips // 2,)),
        ],
        compiler_params=pltpu.CompilerParams(
            collective_id=0, has_side_effects=True, vmem_limit_bytes=56 * 1024 * 1024
        ),
    )(
        queries,
        new_token_key_value,
        key_value_cache.reshape(tokens, key_value_cache.shape[2]),
        row_page_table,
        lengths,
        output_weight_matrix,
        row_adapter_index.reshape(rows),
        adapter_storage_index,
        adapter_down_factor.reshape(rank, features),
        adapter_up_factor.reshape(rank, features),
    )


def attend_rows(queries, new_token_key_value, gathered_pages, lengths):
    local_rows = queries.shape[0]
    token_count = MAXP * PAGE
    group_size = QUERY_HEADS // KVH
    grouped = queries.reshape(local_rows, KVH, group_size, HEAD_SIZE)
    cached = gathered_pages.reshape(local_rows, token_count, KVH, 2, HEAD_SIZE)
    fresh = new_token_key_value.reshape(local_rows, KVH, 2, HEAD_SIZE)
    scale_factor = HEAD_SIZE ** (-0.5)
    scores = (
        jnp.einsum(
            "rkgh,rlkh->rkgl", grouped, cached[:, :, :, 0, :], preferred_element_type=jnp.float32
        )
        * scale_factor
    )
    fresh_score = (
        jnp.einsum("rkgh,rkh->rkg", grouped, fresh[:, :, 0, :], preferred_element_type=jnp.float32)
        * scale_factor
    )
    position = jnp.arange(token_count, dtype=jnp.int32)
    visible = position[None, :] < lengths[:, None]
    scores = jnp.where(visible[:, None, None, :], scores, -1e30)
    row_max = jnp.maximum(jnp.max(scores, axis=-1), fresh_score)
    cached_exp = jnp.exp(scores - row_max[..., None])
    fresh_exp = jnp.exp(fresh_score - row_max)
    total = jnp.sum(cached_exp, axis=-1) + fresh_exp
    weights = (cached_exp / total[..., None]).astype(jnp.bfloat16)
    fresh_weight = (fresh_exp / total).astype(jnp.bfloat16)
    output = jnp.einsum(
        "rkgl,rlkh->rkgh", weights, cached[:, :, :, 1, :], preferred_element_type=jnp.float32
    )
    output = output + fresh_weight.astype(jnp.float32)[..., None] * fresh[:, :, None, 1, :].astype(
        jnp.float32
    )
    return output.reshape(local_rows, QUERY_HEADS * HEAD_SIZE).astype(jnp.bfloat16)


def body(
    queries,
    new_token_key_value,
    key_value_cache,
    row_page_table,
    lengths,
    output_weight_matrix,
    row_adapter_index,
    adapter_storage_index,
    adapter_down_factor,
    adapter_up_factor,
):
    gathered_pages = key_value_cache[row_page_table]
    attention_output = attend_rows(queries, new_token_key_value, gathered_pages, lengths)
    head_rows = lax.all_to_all(attention_output, "tp", split_axis=1, concat_axis=0, tiled=True)
    partial_value = jnp.dot(head_rows, output_weight_matrix, preferred_element_type=jnp.float32)
    base_projection = lax.psum_scatter(partial_value, "tp", scatter_dimension=1, tiled=True)
    row_adapter = row_adapter_index[:, 0]
    row_owner = adapter_storage_index[row_adapter]
    down_slices, up_slices = (
        lax.all_to_all(adapter_down_factor, "tp", split_axis=2, concat_axis=0, tiled=True),
        lax.all_to_all(adapter_up_factor, "tp", split_axis=2, concat_axis=0, tiled=True),
    )
    picked = down_slices[row_owner]
    partial_low = jnp.einsum("rh,rkh->rk", head_rows, picked, preferred_element_type=jnp.float32)
    reduced_output = lax.psum(partial_low, "tp").astype(jnp.bfloat16)
    adapter_term = jnp.einsum(
        "rk,rkd->rd", reduced_output, up_slices[row_owner], preferred_element_type=jnp.float32
    )
    adapter_delta = (adapter_scale * adapter_term).astype(jnp.bfloat16)
    return (base_projection + adapter_delta.astype(jnp.float32)).astype(jnp.bfloat16)


def solution(mesh):
    in_specs = (
        P(("parts", "tp"), None),
        P(("parts", "tp"), None),
        P(("parts", "tp"), None, None),
        P(("parts", "tp"), None),
        P(("parts", "tp")),
        P("tp", None),
        P("parts", None),
        P("parts"),
        P(("parts", "tp"), None, None),
        P(("parts", "tp"), None, None),
    )
    out_specs = P("parts", "tp")
    n = mesh.shape["tp"]
    run = functools.partial(fused_body, n) if n == 16 else body
    return jax.shard_map(run, mesh=mesh, in_specs=in_specs, out_specs=out_specs, check_vma=False)
```

```python
import functools

import jax
import jax.numpy as jnp
from jax import lax
from jax.experimental import pallas as pl
from jax.experimental.pallas import tpu as pltpu
from jax.sharding import PartitionSpec as P

QUERY_HEADS = 128
KVH = 8
HEAD_SIZE = 128
PAGE = 16
MAXP = 32
CAP = 4
MESH = pl.DeviceIdType.MESH


adapter_scale = 2.0


def fused_kernel(
    n,
    q_ref,
    new_ref,
    kv_hbm,
    table_ref,
    len_ref,
    w_hbm,
    adapter_ref,
    storage_ref,
    down_hbm,
    up_hbm,
    out_ref,
    kv,
    w,
    down,
    up,
    bias,
    qs,
    send1,
    recv1,
    xf,
    xs,
    send2,
    recv2,
    send3,
    recv3,
    psend,
    precv,
    keep,
    ysend,
    yrecv,
    isend,
    irecv,
    kv_sem,
    w_sem,
    f_sem,
    ss1,
    rs1,
    ss2,
    rs2,
    ss3,
    rs3,
    pss,
    prs,
    yss,
    yrs,
    iss,
    irs,
):
    f32, bf16, i32 = jnp.float32, jnp.bfloat16, jnp.int32
    part = lax.axis_index("parts")
    me = lax.axis_index("tp")
    core = lax.rem(me, 2)
    chip = lax.div(me, 2)
    depth, across = lax.div(chip, 2), lax.rem(chip, 2)
    chips = n // 2
    depths = chips // 2
    tokens = kv.shape[1]
    rows = xs.shape[0]
    width = xs.shape[1]

    def to_depth(k):
        shift = jnp.where(k == 0, 2, jnp.where(k == 1, 1, jnp.where(k == 2, 3, 0)))
        return lax.rem(depth + shift, depths)

    def to_chip(k):
        near = lax.div(k, depths) == 1
        return to_depth(lax.rem(k, depths)) * 2 + jnp.where(near, across, 1 - across)

    def kv_copy(g):
        return pltpu.make_async_copy(
            kv_hbm.at[:, pl.ds(pl.multiple_of(g * 256, 256), 256)], kv.at[g], kv_sem.at[g]
        )

    def w_copy(i):
        k, own = lax.div(i, 2), lax.rem(i, 2)
        device = to_chip(k) * 2 + jnp.where(own == 1, core, 1 - core)
        start = pl.multiple_of(device * width, width)
        return pltpu.make_async_copy(w_hbm.at[:, pl.ds(start, width)], w.at[i], w_sem.at[i])

    down_copy = pltpu.make_async_copy(down_hbm, down, f_sem.at[0])
    up_copy = pltpu.make_async_copy(up_hbm, up, f_sem.at[1])

    def loop(low, high, body):
        lax.fori_loop(low, high, lambda i, c: (body(i), c)[1], 0)

    def to_peers(body):
        def one(d):
            @pl.when(d != me)
            def _():
                body(d)

        loop(0, n, one)

    loop(0, KVH, lambda g: kv_copy(g).start())
    barrier = pltpu.get_barrier_semaphore()
    to_peers(
        lambda d: pl.semaphore_signal(barrier, inc=1, device_id=(part, d), device_id_type=MESH)
    )

    loop(0, 8, lambda i: w_copy(i).start())
    down_copy.start()
    up_copy.start()
    loop(8, n, lambda i: w_copy(i).start())

    page = lax.broadcasted_iota(i32, (MAXP, tokens), 1) // PAGE
    slot_at = lax.broadcasted_iota(i32, (MAXP, tokens), 0)
    offset = lax.broadcasted_iota(i32, (MAXP, tokens), 1) % PAGE
    position = (slot_at * PAGE + offset).astype(f32)
    eye = lax.broadcasted_iota(i32, (MAXP, MAXP), 0) == lax.broadcasted_iota(i32, (MAXP, MAXP), 1)
    table = table_ref[...].astype(f32)
    seen = []
    for r in range(2):
        pages = jnp.sum(jnp.where(eye, table[r : r + 1, :], 0.0), axis=1, keepdims=True)
        length = len_ref[r].astype(f32)
        hit = jnp.where((page.astype(f32) == pages) & (position < length), 1.0, 0.0)
        seen.append(jnp.sum(hit, axis=0, keepdims=True))
    row_of = (lax.broadcasted_iota(i32, (32, 1), 0) // 8) % 2
    visible = jnp.where(row_of == 0, seen[0], seen[1])
    bias[...] = jnp.where(visible > 0.5, 0.0, -1e30)

    for h in range(n * 8):
        at_row = (h // 8) * 16 + h % 8
        qs[pl.ds(at_row, 2, stride=8), :] = q_ref[:, h * 128 : h * 128 + 128].astype(f32)

    def send1_copy(d):
        return pltpu.make_async_remote_copy(
            src_ref=send1.at[d],
            dst_ref=recv1.at[me],
            send_sem=ss1.at[d],
            recv_sem=rs1.at[me],
            device_id=(part, d),
            device_id_type=MESH,
        )

    scale = HEAD_SIZE ** (-0.5)

    def attend(g):
        kv_copy(g).wait()
        query = qs[pl.ds(pl.multiple_of(g * 32, 32), 32), :].astype(bf16)
        keys = kv[g, :, 0:128]
        scores = lax.dot_general(query, keys, (((1,), (1,)), ((), ())), preferred_element_type=f32)
        scores = scores * scale + bias[...]
        fresh = new_ref[:, pl.ds(pl.multiple_of(g * 256, 256), 256)].astype(f32)
        fresh = jnp.where(row_of == 0, fresh[0:1], fresh[1:2])
        fresh_score = jnp.sum(query.astype(f32) * fresh[:, :128], axis=1, keepdims=True) * scale
        top = jnp.maximum(jnp.max(scores, axis=1, keepdims=True), fresh_score)
        grown = jnp.exp(scores - top)
        fresh_grown = jnp.exp(fresh_score - top)
        inverse = 1.0 / (jnp.sum(grown, axis=1, keepdims=True) + fresh_grown)
        weights = (grown * inverse).astype(bf16)
        fresh_weight = (fresh_grown * inverse).astype(bf16).astype(f32)
        attended = jnp.dot(weights, kv[g, :, 128:256], preferred_element_type=f32)
        attended = (attended + fresh_weight * fresh[:, 128:]).astype(bf16)
        for half in range(2):
            d = g * 2 + half
            send1[d] = attended[half * 16 : half * 16 + 16]

    loop(0, KVH, attend)
    pl.semaphore_wait(barrier, n - 1)
    to_peers(lambda d: send1_copy(d).start())

    lane = lax.broadcasted_iota(i32, (rows, 128), 1) % rows
    sub = lax.broadcasted_iota(i32, (rows, 128), 0)
    owner_row = jnp.zeros((rows, 128), i32)
    owner_column = jnp.zeros((rows, 128), i32)
    for r in range(rows):
        owner = storage_ref[adapter_ref[r]]
        owner_row = jnp.where(lane == r, owner, owner_row)
        owner_column = jnp.where(sub == r, owner, owner_column)
    same = owner_row == owner_column
    first = lax.broadcasted_iota(i32, (rows, 128), 1) < rows
    rank_row = jnp.sum(jnp.where(same & (sub < lane), 1.0, 0.0), axis=0, keepdims=True)
    rank_column = jnp.sum(jnp.where(same & (lane < sub) & first, 1.0, 0.0), axis=1, keepdims=True)
    slot_row = owner_row[0:1].astype(f32) * CAP + rank_row
    slot_column = owner_column[:, 0:1].astype(f32) * CAP + rank_column
    at = lax.broadcasted_iota(i32, (n * 16, 128), 0)
    quarter_at = lax.broadcasted_iota(i32, (n * 16, 128), 1) // rows
    wanted = ((at // 16) * CAP + at % CAP).astype(f32)
    place = jnp.where((wanted == slot_row) & ((at // CAP) % 4 == quarter_at), 1.0, 0.0).astype(bf16)

    recv1[me] = send1[me]
    to_peers(lambda d: pltpu.make_async_remote_copy(
        src_ref=send1.at[d],
        dst_ref=recv1.at[d],
        send_sem=ss1.at[d],
        recv_sem=rs1.at[d],
        device_id=(part, d),
        device_id_type=MESH,
    ).wait_recv())
    xf[...] = recv1[...].reshape(n * 16, 128).astype(f32)
    x = jnp.concatenate([xf[pl.ds(h, rows, stride=8), :] for h in range(8)], axis=1).astype(bf16)
    xs[...] = x

    def copy_of(send, recv, ss, rs, d, landing):
        return pltpu.make_async_remote_copy(
            src_ref=send.at[d],
            dst_ref=recv.at[landing],
            send_sem=ss.at[d],
            recv_sem=rs.at[landing],
            device_id=(part, d),
            device_id_type=MESH,
        )

    stacked = jnp.concatenate([x[:, i * 256 : i * 256 + 256] for i in range(4)], axis=0)
    picked = jnp.dot(place, stacked, preferred_element_type=f32).astype(bf16)
    send2[...] = picked.reshape(n, 16, 256)
    to_peers(lambda d: copy_of(send2, recv2, ss2, rs2, d, me).start())
    recv2[me] = send2[me]

    def partner_copy(k):
        return pltpu.make_async_remote_copy(
            src_ref=psend.at[k],
            dst_ref=precv.at[k],
            send_sem=pss.at[k],
            recv_sem=prs.at[k],
            device_id=(part, chip * 2 + 1 - core),
            device_id_type=MESH,
        )

    def across_copy(k):
        return pltpu.make_async_remote_copy(
            src_ref=ysend.at[k],
            dst_ref=yrecv.at[k],
            send_sem=yss.at[k],
            recv_sem=yrs.at[k],
            device_id=(part, (depth * 2 + 1 - across) * 2 + core),
            device_id_type=MESH,
        )

    def depth_copy(k):
        return pltpu.make_async_remote_copy(
            src_ref=isend.at[k],
            dst_ref=irecv.at[k],
            send_sem=iss.at[k],
            recv_sem=irs.at[k],
            device_id=(part, (to_depth(k) * 2 + across) * 2 + core),
            device_id_type=MESH,
        )

    def multiply(k):
        for own, into in ((0, psend), (1, keep)):
            w_copy(k * 2 + own).wait()
            for c in range(0, width, 512):
                into[k, :, c : c + 512] = jnp.dot(
                    xs[...], w[k * 2 + own, :, c : c + 512], preferred_element_type=f32
                )
            if own == 0:
                partner_copy(k).start()

    def sum_far(k):
        partner_copy(k).wait_recv()
        ysend[k] = (keep[k] + precv[k]).astype(bf16)
        across_copy(k).start()

    def sum_near(k):
        partner_copy(depths + k).wait_recv()
        across_copy(k).wait_recv()
        return keep[depths + k] + precv[depths + k] + yrecv[k].astype(f32)

    def send_depth(k):
        isend[k] = sum_near(k).astype(bf16)
        depth_copy(k).start()

    def far_step(k):
        multiply(k)
        sum_far(k - 1)

    def near_step(k):
        multiply(depths + k)
        send_depth(k - 1)

    multiply(0)
    loop(1, depths + 1, far_step)
    loop(1, depths - 1, near_step)

    multiply(chips - 1)
    send_depth(depths - 2)

    down_copy.wait()
    up_copy.wait()
    to_peers(lambda d: copy_of(send2, recv2, ss2, rs2, d, d).wait_recv())
    quarter = lax.broadcasted_iota(i32, (16, 256), 0) // CAP

    def reduce_one(s, total):
        piece = recv2[s].astype(f32)
        spread = jnp.concatenate(
            [jnp.where(quarter == i, piece, 0.0) for i in range(4)], axis=1
        ).astype(bf16)
        factor = down[:, pl.ds(pl.multiple_of(s * width, width), width)]
        return total + lax.dot_general(
            spread, factor, (((1,), (1,)), ((), ())), preferred_element_type=f32
        )

    total = lax.fori_loop(0, n, reduce_one, jnp.zeros((16, down.shape[0]), f32), unroll=4)
    summed = total[0:4] + total[4:8] + total[8:12] + total[12:16]
    reduced = jnp.concatenate([summed] * 4, axis=0).astype(bf16)

    def raise_four(start):
        for d in [start * 4 + i for i in range(4)]:
            factor = up[:, pl.ds(pl.multiple_of(d * width, width), width)]
            term = adapter_scale * jnp.dot(reduced, factor, preferred_element_type=f32)
            piece = jnp.zeros((16, 256), f32)
            for i in range(4):
                piece = jnp.where(quarter == i, term[:, i * 256 : i * 256 + 256], piece)
            send3[d] = piece.astype(bf16)
        for d in [start * 4 + i for i in range(4)]:

            @pl.when(d != me)
            def _():
                copy_of(send3, recv3, ss3, rs3, d, me).start()

    loop(0, n // 4, raise_four)
    recv3[me] = send3[me]
    result = sum_near(depths - 1)
    for k in range(depths - 1):
        depth_copy(k).wait_recv()
        result = result + irecv[k].astype(f32)

    to_peers(lambda d: copy_of(send3, recv3, ss3, rs3, d, d).wait_recv())
    back = lax.broadcasted_iota(i32, (rows, n * 16), 1)
    named = ((back // 16) * CAP + back % CAP).astype(f32) == slot_column
    deltas = recv3[...].reshape(n * 16, 256)
    result = result + jnp.concatenate(
        [
            jnp.dot(
                jnp.where(named & ((back // CAP) % 4 == i), 1.0, 0.0).astype(bf16),
                deltas,
                preferred_element_type=f32,
            )
            for i in range(4)
        ],
        axis=1,
    )
    out_ref[...] = result.astype(bf16)

    def sent(d):
        copy_of(send1, recv1, ss1, rs1, d, me).wait_send()
        copy_of(send2, recv2, ss2, rs2, d, me).wait_send()
        copy_of(send3, recv3, ss3, rs3, d, me).wait_send()

    to_peers(sent)
    loop(0, chips, lambda k: partner_copy(k).wait_send())
    loop(0, depths, lambda k: across_copy(k).wait_send())
    loop(0, depths - 1, lambda k: depth_copy(k).wait_send())


def fused_body(
    n,
    queries,
    new_token_key_value,
    key_value_cache,
    row_page_table,
    lengths,
    output_weight_matrix,
    row_adapter_index,
    adapter_storage_index,
    adapter_down_factor,
    adapter_up_factor,
):
    rows = row_adapter_index.shape[0]
    width = output_weight_matrix.shape[0]
    tokens = key_value_cache.shape[0] * PAGE
    rank = adapter_down_factor.shape[1]
    features = queries.shape[1]
    chips = n // 2
    bf16, f32 = jnp.bfloat16, jnp.float32
    vmem = pl.BlockSpec(memory_space=pltpu.VMEM)
    smem = pl.BlockSpec(memory_space=pltpu.SMEM)
    hbm = pl.BlockSpec(memory_space=pl.ANY)
    dma = pltpu.SemaphoreType.DMA
    return pl.pallas_call(
        functools.partial(fused_kernel, n),
        out_shape=jax.ShapeDtypeStruct((rows, width), bf16),
        in_specs=[vmem, vmem, hbm, vmem, smem, hbm, smem, smem, hbm, hbm],
        out_specs=vmem,
        scratch_shapes=[
            pltpu.VMEM((KVH, tokens, 256), bf16),
            pltpu.VMEM((n, width, width), bf16),
            pltpu.VMEM((rank, features), bf16),
            pltpu.VMEM((rank, features), bf16),
            pltpu.VMEM((32, tokens), f32),
            pltpu.VMEM((n * 16, 128), f32),
            pltpu.VMEM((n, 16, 128), bf16),
            pltpu.VMEM((n, 16, 128), bf16),
            pltpu.VMEM((n * 16, 128), f32),
            pltpu.VMEM((rows, width), bf16),
            pltpu.VMEM((n, 16, 256), bf16),
            pltpu.VMEM((n, 16, 256), bf16),
            pltpu.VMEM((n, 16, 256), bf16),
            pltpu.VMEM((n, 16, 256), bf16),
            pltpu.VMEM((chips, rows, width), f32),
            pltpu.VMEM((chips, rows, width), f32),
            pltpu.VMEM((chips, rows, width), f32),
            pltpu.VMEM((chips // 2, rows, width), bf16),
            pltpu.VMEM((chips // 2, rows, width), bf16),
            pltpu.VMEM((chips // 2, rows, width), bf16),
            pltpu.VMEM((chips // 2, rows, width), bf16),
            dma((KVH,)),
            dma((n,)),
            dma((2,)),
            dma((n,)),
            dma((n,)),
            dma((n,)),
            dma((n,)),
            dma((n,)),
            dma((n,)),
            dma((chips,)),
            dma((chips,)),
            dma((chips // 2,)),
            dma((chips // 2,)),
            dma((chips // 2,)),
            dma((chips // 2,)),
        ],
        compiler_params=pltpu.CompilerParams(
            collective_id=0, has_side_effects=True, vmem_limit_bytes=56 * 1024 * 1024
        ),
    )(
        queries,
        new_token_key_value,
        key_value_cache.reshape(tokens, key_value_cache.shape[2]),
        row_page_table,
        lengths,
        output_weight_matrix,
        row_adapter_index.reshape(rows),
        adapter_storage_index,
        adapter_down_factor.reshape(rank, features),
        adapter_up_factor.reshape(rank, features),
    )


def attend_rows(queries, new_token_key_value, gathered_pages, lengths):
    local_rows = queries.shape[0]
    token_count = MAXP * PAGE
    group_size = QUERY_HEADS // KVH
    grouped = queries.reshape(local_rows, KVH, group_size, HEAD_SIZE)
    cached = gathered_pages.reshape(local_rows, token_count, KVH, 2, HEAD_SIZE)
    fresh = new_token_key_value.reshape(local_rows, KVH, 2, HEAD_SIZE)
    scale_factor = HEAD_SIZE ** (-0.5)
    scores = (
        jnp.einsum(
            "rkgh,rlkh->rkgl", grouped, cached[:, :, :, 0, :], preferred_element_type=jnp.float32
        )
        * scale_factor
    )
    fresh_score = (
        jnp.einsum("rkgh,rkh->rkg", grouped, fresh[:, :, 0, :], preferred_element_type=jnp.float32)
        * scale_factor
    )
    position = jnp.arange(token_count, dtype=jnp.int32)
    visible = position[None, :] < lengths[:, None]
    scores = jnp.where(visible[:, None, None, :], scores, -1e30)
    row_max = jnp.maximum(jnp.max(scores, axis=-1), fresh_score)
    cached_exp = jnp.exp(scores - row_max[..., None])
    fresh_exp = jnp.exp(fresh_score - row_max)
    total = jnp.sum(cached_exp, axis=-1) + fresh_exp
    weights = (cached_exp / total[..., None]).astype(jnp.bfloat16)
    fresh_weight = (fresh_exp / total).astype(jnp.bfloat16)
    output = jnp.einsum(
        "rkgl,rlkh->rkgh", weights, cached[:, :, :, 1, :], preferred_element_type=jnp.float32
    )
    output = output + fresh_weight.astype(jnp.float32)[..., None] * fresh[:, :, None, 1, :].astype(
        jnp.float32
    )
    return output.reshape(local_rows, QUERY_HEADS * HEAD_SIZE).astype(jnp.bfloat16)


def body(
    queries,
    new_token_key_value,
    key_value_cache,
    row_page_table,
    lengths,
    output_weight_matrix,
    row_adapter_index,
    adapter_storage_index,
    adapter_down_factor,
    adapter_up_factor,
):
    gathered_pages = key_value_cache[row_page_table]
    attention_output = attend_rows(queries, new_token_key_value, gathered_pages, lengths)
    head_rows = lax.all_to_all(attention_output, "tp", split_axis=1, concat_axis=0, tiled=True)
    partial_value = jnp.dot(head_rows, output_weight_matrix, preferred_element_type=jnp.float32)
    base_projection = lax.psum_scatter(partial_value, "tp", scatter_dimension=1, tiled=True)
    row_adapter = row_adapter_index[:, 0]
    row_owner = adapter_storage_index[row_adapter]
    down_slices, up_slices = (
        lax.all_to_all(adapter_down_factor, "tp", split_axis=2, concat_axis=0, tiled=True),
        lax.all_to_all(adapter_up_factor, "tp", split_axis=2, concat_axis=0, tiled=True),
    )
    picked = down_slices[row_owner]
    partial_low = jnp.einsum("rh,rkh->rk", head_rows, picked, preferred_element_type=jnp.float32)
    reduced_output = lax.psum(partial_low, "tp").astype(jnp.bfloat16)
    adapter_term = jnp.einsum(
        "rk,rkd->rd", reduced_output, up_slices[row_owner], preferred_element_type=jnp.float32
    )
    adapter_delta = (adapter_scale * adapter_term).astype(jnp.bfloat16)
    return (base_projection + adapter_delta.astype(jnp.float32)).astype(jnp.bfloat16)


def solution(mesh):
    in_specs = (
        P(("parts", "tp"), None),
        P(("parts", "tp"), None),
        P(("parts", "tp"), None, None),
        P(("parts", "tp"), None),
        P(("parts", "tp")),
        P("tp", None),
        P("parts", None),
        P("parts"),
        P(("parts", "tp"), None, None),
        P(("parts", "tp"), None, None),
    )
    out_specs = P("parts", "tp")
    n = mesh.shape["tp"]
    run = functools.partial(fused_body, n) if n == 16 else body
    return jax.shard_map(run, mesh=mesh, in_specs=in_specs, out_specs=out_specs, check_vma=False)
```
